32 devices in a mesh: vox: 16 (over z, x, core), echo: 2 (over y).
Axes of the slice: x: 2, y: 2, z: 4, core: 2. Of those that a mesh axis runs over, the one named last changes fastest.
Arguments:
- acquired: bfloat16 [131072, 128], P(('vox', 'echo')), may hold values from -6 to 6
- owner: int32 [131072, 1], P(('vox', 'echo')), may hold values from 0 to 15; in each aligned block of 4096 rows (0 to 4095, 4096 to 8191, ...) at most 1024 rows name the same one
- slot: int32 [131072, 1], P(('vox', 'echo')), may hold values from 0 to 32767
- sampled: int32 [4096, 256], P('vox', 'echo'), may hold values 0 or 1
- left_panel: bfloat16 [128, 32], replicated, may hold values from -0.5 to 0.5
- right_panel: bfloat16 [256, 32], P('echo'), may hold values from -0.75 to 0.75
Outputs:
- coefficients: bfloat16 [4096, 1024], P(('vox', 'echo'))
The draws below stay inside these ranges and needn't reach their ends.
Inputs may be any that keep to these rules, and one draw needn't show every extreme that they name: Among the rows of one device, no owner is named more than 1024 times, a bound that some block reaches.
All inputs are finite; a program needn't handle non-finite values. No bound on the sum of `sampled` on one device may be relied on, other than what follows from the above.
Results may differ from the reference program's by a relative error of at most 0.005.
Values may be sent and summed in bfloat16 or wider, within the bound.
No kernel may reach another device: no remote copies, remote signals or barrier semaphores. Data moves between devices by JAX's collectives and lax.ppermute only.
A program may use at most 64 MiB of HBM per device.

```python
import math
import jax
import jax.numpy as jnp
import numpy as np
from jax import lax

B = 128
E = 256
R = 32
VOX_DEV = 256
ROWS_DEV = 4096
E_DEV = 128
CAP = 1024
VOX_TOTAL = 4096
ROWS_TOTAL = 131072
N_VOX = 16
N_ECHO = 2


def with_ends(entries, rng, least, top_value):
    shape = entries.shape
    spot = [jax.random.randint(jax.random.fold_in(rng, axis), (), 0, shape[axis]) for axis in range(len(shape))]
    entries = entries.at[tuple(spot)].set(least)
    longest = shape.index(max(shape))
    spot[longest] = (spot[longest] + 1) % shape[longest]
    return entries.at[tuple(spot)].set(top_value)


def block_levels(stream_key, dims, pieces, least, top_value):
    level, own = 1.0, jax.random.fold_in(stream_key, 6)
    for axis_at, shards_of in pieces:
        heights = jnp.exp(jax.random.uniform(jax.random.fold_in(own, axis_at), (shards_of,), jnp.float32, least / len(pieces), top_value / len(pieces)))
        level = level * jnp.repeat(heights, dims[axis_at] // shards_of).reshape([-1 if axis == axis_at else 1 for axis in range(len(dims))])
    return level


def shared_out(rng, own, number, rows, number_of, top, most, slope):
    ranking = jax.random.permutation(rng, number_of)
    crowded, common = portions_of(number_of, rows * top, most, slope, True), portions_of(number_of, rows * top, most, slope, False)
    places = jnp.arange(number_of)

    def named(lengths, offset_by):
        used = int((lengths > 0).sum())
        fixed = max(1, used // 4)
        moved = fixed + (places - fixed + offset_by * (used - fixed)) % max(1, number_of - fixed)
        return jnp.zeros((number_of,), jnp.int32).at[ranking[jnp.where(places < fixed, places, moved)]].set(jnp.asarray(lengths, jnp.int32))

    lengths = jnp.where(number % 4 == 0, named(crowded, number // 4), named(common, number - number // 4 - 1))
    mixed = jax.random.permutation(jax.random.fold_in(own, 3), number_of)
    source_of, taker = mixed[0:number_of // 2 * 2:2], mixed[1:number_of // 2 * 2:2]
    margin = jnp.minimum(lengths[source_of] - 1, most - lengths[taker]) // 2
    margin = jnp.where((source_of == ranking[0]) | (taker == ranking[0]) | (lengths[taker] == 0), 0, jnp.maximum(margin, 0))
    moved = jax.random.randint(jax.random.fold_in(own, 4), (number_of // 2,), 0, 1 << 20) % (margin + 1)
    lengths = lengths.at[source_of].add(-moved).at[taker].add(moved)
    members = jnp.searchsorted(jnp.cumsum(lengths), jnp.arange(rows * top), side="right").astype(jnp.int32)
    listing = members.reshape(top, rows).T
    listing = listing[jax.random.permutation(jax.random.fold_in(own, 1), rows)]
    offset_by = jax.random.randint(jax.random.fold_in(own, 2), (rows, 1), 0, top)
    return jnp.take_along_axis(listing, (jnp.arange(top)[None, :] + offset_by) % top, axis=1)


def portions_of(number_of, total, reach, lean, full):
    loads = [(1 << 20) // math.isqrt(rank ** lean) + 1 for rank in range(1, number_of + 1)]
    largest = reach if full else min(reach, max(-(-total // number_of), total * loads[0] // sum(loads)))
    least = 1 if total - largest >= number_of - 1 else 0
    holding, spare = [largest] + [least] * (number_of - 1), total - largest - least * (number_of - 1)
    while spare > 0:
        free = [i for i in range(1, number_of) if holding[i] < largest] or [i for i in range(1, number_of) if holding[i] < reach]
        pool, left = sum([loads[i] for i in free]), spare
        for i in free:
            more = min(reach - holding[i], max(1, left * loads[i] // pool), spare)
            holding[i] = holding[i] + more
            spare = spare - more
    return np.array(holding)


def bell_draw(rng, shape, deviation, bound, pieces=(), kind=jnp.bfloat16):
    values = deviation * jax.random.normal(rng, shape, jnp.float32)
    if pieces:
        values = values * block_levels(rng, shape, pieces, -0.22, 0.18)
    return jnp.clip(values, -bound, bound).astype(kind)


def setup_inputs(seed: int = 0) -> dict:
    key_of = jax.random.split(jax.random.key(seed), 7)
    acquired = bell_draw(key_of[0], (ROWS_TOTAL, B), 1.0, 6.0, ((0, 32),))
    owner_keys = jax.random.split(jax.random.fold_in(key_of[1], 1), ROWS_TOTAL // ROWS_DEV)
    owner_turns = jax.random.permutation(jax.random.fold_in(key_of[1], 3), ROWS_TOTAL // ROWS_DEV)
    owner = jax.vmap(lambda own, number: shared_out(jax.random.fold_in(key_of[1], 2), own, number, ROWS_DEV, N_VOX, 1, CAP, 2))(owner_keys, owner_turns).reshape((ROWS_TOTAL, 1))
    slot = with_ends(jax.random.randint(key_of[2], (ROWS_TOTAL, 1), 0, VOX_DEV * E_DEV), jax.random.fold_in(key_of[2], 1), 0, (VOX_DEV * E_DEV) - 1).astype(jnp.int32)
    sampled = with_ends((jax.random.randint(key_of[3], (VOX_TOTAL, E), 0, 2) < 1).astype(jnp.int32), jax.random.fold_in(key_of[3], 1), 0, 1)
    left_panel = bell_draw(key_of[4], (B, R), B ** -0.5, 0.5)
    right_panel = bell_draw(key_of[5], (E, R), (E // 4) ** -0.5, 0.75, ((0, 2),))
    return dict(acquired=acquired, owner=owner, slot=slot, sampled=sampled, left_panel=left_panel, right_panel=right_panel)


def reference(acquired, owner, slot, sampled, left_panel, right_panel):
    reduced = jnp.dot(acquired, left_panel, preferred_element_type=jnp.float32).astype(jnp.bfloat16)
    row_index = jnp.arange(ROWS_TOTAL, dtype=jnp.int32)
    block = row_index // ROWS_DEV
    slot_flat = slot[:, 0].astype(jnp.int32)
    voxel = owner[:, 0].astype(jnp.int32) * VOX_DEV + slot_flat // E_DEV
    echo_index = (block % N_ECHO) * E_DEV + slot_flat % E_DEV
    segment = voxel * E + echo_index
    filled = jax.ops.segment_sum(reduced.astype(jnp.float32), segment, num_segments=VOX_TOTAL * E)
    filled = filled.reshape(VOX_TOTAL, E, R) * sampled.astype(jnp.float32)[:, :, None]
    core = jnp.einsum("ver,es->vrs", filled, right_panel.astype(jnp.float32), precision=lax.Precision.HIGHEST)
    return core.reshape(VOX_TOTAL, R * R).astype(jnp.bfloat16)
```

```python
import functools

import jax
import jax.numpy as jnp
from jax import lax
from jax.experimental import pallas as pl
from jax.experimental.pallas import tpu as pltpu
from jax.sharding import PartitionSpec as P

LANES = 128
CHUNK = 512
FINE = 16
BF16 = jnp.bfloat16
F32 = jnp.float32
I32 = jnp.int32


def nt_dot(lhs, rhs):
    return lax.dot_general(
        lhs, rhs, (((1,), (1,)), ((), ())), preferred_element_type=F32
    )


def nn_dot(lhs, rhs):
    return lax.dot_general(
        lhs, rhs, (((1,), (0,)), ((), ())), preferred_element_type=F32
    )


def pack_kernel(
    owners, capacity, echo_local, me_ref, acquired_ref, owner_ref, slot_ref, left_ref,
    out_ref, place_ref, feature_ref, id_ref,
):
    rows = acquired_ref.shape[0]
    rank = left_ref.shape[0]
    chunks = rows // CHUNK
    groups = capacity // LANES
    me = me_ref[0]
    owner_range = lax.broadcasted_iota(I32, (owners, CHUNK), 0)
    hots = []
    for j in range(chunks):
        relative = owner_ref[:, j * CHUNK : (j + 1) * CHUNK] ^ me
        hots.append((owner_range == relative).astype(F32))
    hot = jnp.concatenate(hots, axis=0)
    before = lax.broadcasted_iota(I32, (CHUNK, CHUNK), 0) < lax.broadcasted_iota(
        I32, (CHUNK, CHUNK), 1
    )
    prefix = nn_dot(hot.astype(BF16), before.astype(F32).astype(BF16))
    carry = jnp.zeros((owners, 1), F32)
    for j in range(chunks):
        part = prefix[j * owners : (j + 1) * owners]
        place = jnp.sum((part + carry) * hots[j], axis=0, keepdims=True)
        place_ref[j] = place.astype(I32)
        carry = carry + jnp.sum(hots[j], axis=1, keepdims=True)
    feature_ref[...] = jnp.zeros_like(feature_ref)
    id_ref[...] = jnp.zeros_like(id_ref)
    left = left_ref[...]
    lane_range = lax.broadcasted_iota(I32, (LANES, CHUNK), 0)
    group_range = lax.broadcasted_iota(I32, (8, CHUNK), 0)

    def step(j, _):
        at = pl.multiple_of(j * CHUNK, CHUNK)
        reduced = nt_dot(left, acquired_ref[pl.ds(at, CHUNK), :]).astype(BF16)
        relative = owner_ref[:, pl.ds(at, CHUNK)] ^ me
        slot = slot_ref[:, pl.ds(at, CHUNK)]
        place = place_ref[j]
        group = place // LANES
        lane_hot = (lane_range == place % LANES).astype(F32).astype(BF16)
        group_b = jnp.broadcast_to(group.astype(F32), (LANES, CHUNK)).astype(BF16)
        place_hot = jnp.concatenate(
            [
                jnp.where(group_b == BF16(g), lane_hot, BF16(0))
                for g in range(groups)
            ],
            axis=0,
        )
        here = group_range == group
        voxel = jnp.where(here, (slot // echo_local).astype(F32), 0.0)
        echo = jnp.where(here, (slot % echo_local).astype(F32), 0.0)
        ids = jnp.concatenate([voxel, echo], axis=0).astype(BF16)
        owner_b = jnp.broadcast_to(relative.astype(F32), (rank, CHUNK)).astype(BF16)
        owner_c = owner_b[:16]
        spread = jnp.concatenate(
            [jnp.where(owner_b == BF16(o), reduced, BF16(0)) for o in range(owners)],
            axis=0,
        )
        spread_ids = jnp.concatenate(
            [jnp.where(owner_c == BF16(o), ids, BF16(0)) for o in range(owners)],
            axis=0,
        )
        feature_ref[...] += nt_dot(spread, place_hot)
        id_ref[...] += nt_dot(spread_ids, lane_hot)
        return 0

    lax.fori_loop(0, chunks, step, 0)
    for o in range(owners):
        for g in range(groups):
            out_ref[o, g * rank : (g + 1) * rank, :] = feature_ref[
                o * rank : (o + 1) * rank, g * LANES : (g + 1) * LANES
            ].astype(BF16)
        out_ref[o, groups * rank :, :] = id_ref[o * 16 : (o + 1) * 16, :].astype(BF16)


def core_kernel(groups, blocks_ref, sampled_ref, right_ref, out_ref, a_ref, b_ref):
    count = blocks_ref.shape[0]
    rank = right_ref.shape[0]
    shares, _, width = out_ref.shape
    echo_local = sampled_ref.shape[1]
    bits = sampled_ref[0:32, :]
    for b in range(1, sampled_ref.shape[0] // 32):
        bits = bits + (sampled_ref[b * 32 : (b + 1) * 32, :] << b)
    table = jnp.concatenate([right_ref[...], bits.astype(F32).astype(BF16)], axis=0)
    echo_range = lax.broadcasted_iota(I32, (echo_local, LANES), 0).astype(F32).astype(BF16)
    bit_range = lax.broadcasted_iota(I32, (32, LANES), 0)
    out_ref[...] = jnp.zeros_like(out_ref)

    def step(s, _):
        ids = blocks_ref[s, groups * rank :, :].astype(F32)
        for g in range(groups):
            feature = blocks_ref[s, g * rank : (g + 1) * rank, :]
            voxel = ids[g : g + 1].astype(I32)
            echo = jnp.broadcast_to(ids[8 + g : 9 + g], (echo_local, LANES)).astype(BF16)
            echo_hot = jnp.where(echo == echo_range, BF16(1), BF16(0))
            found = nn_dot(table, echo_hot)
            word = jnp.sum(
                jnp.where(bit_range == voxel % 32, found[rank:], 0.0),
                axis=0, keepdims=True,
            ).astype(I32)
            mask = ((word >> (voxel // 32)) & 1).astype(F32)
            right = (found[:rank] * mask).astype(BF16)
            low = jnp.broadcast_to((voxel % FINE).astype(F32), (rank, LANES)).astype(BF16)
            high = jnp.broadcast_to((voxel // FINE).astype(F32), (rank, LANES)).astype(BF16)
            at = slice(g * LANES, (g + 1) * LANES)
            for v in range(FINE):
                a_ref[v * rank : (v + 1) * rank, at] = jnp.where(
                    low == BF16(v), feature, BF16(0)
                )
                b_ref[v * rank : (v + 1) * rank, at] = jnp.where(
                    high == BF16(v), right, BF16(0)
                )
        for h in range(shares):
            out_ref[h] += nt_dot(a_ref[...], b_ref[h * width : (h + 1) * width, :])
        return 0

    lax.fori_loop(0, count, step, 0)


def finish_kernel(rank, keep_ref, got_ref, out_ref, sum_ref):
    tiles = keep_ref.shape[1] // LANES
    per = LANES // rank
    block = lax.broadcasted_iota(I32, (FINE, LANES), 1) // rank
    for t in range(tiles):
        sum_ref[...] = (
            keep_ref[:, t * LANES : (t + 1) * LANES]
            + got_ref[:, t * LANES : (t + 1) * LANES].astype(F32)
        )
        for q in range(rank // per):
            rows = [
                sum_ref[pl.ds(q * per + i, FINE, stride=rank), :] for i in range(per)
            ]
            for k in range(per):
                made = None
                for i in range(per):
                    turn = (i - k) % per * rank
                    moved = pltpu.roll(rows[i], turn, 1) if turn else rows[i]
                    made = moved if made is None else jnp.where(block == i, moved, made)
                v = t * per + k
                out_ref[v * FINE : (v + 1) * FINE, q * LANES : (q + 1) * LANES] = (
                    made.astype(BF16)
                )


VMEM = pl.BlockSpec(memory_space=pltpu.VMEM)
SMEM = pl.BlockSpec(memory_space=pltpu.SMEM)
PARAMS = pltpu.CompilerParams(vmem_limit_bytes=48 * 2**20)


def on_device(acquired, owner, slot, sampled, left_panel, right_panel):
    owners = lax.axis_size("vox")
    shares = lax.axis_size("echo")
    rows = acquired.shape[0]
    capacity = 4 * rows // owners
    groups = capacity // LANES
    vox_local, echo_local = sampled.shape
    rank = left_panel.shape[1]
    depth = groups * rank + 16
    width = FINE * rank // shares
    packed = pl.pallas_call(
        functools.partial(pack_kernel, owners, capacity, echo_local),
        out_shape=jax.ShapeDtypeStruct((owners, depth, LANES), BF16),
        in_specs=[SMEM, VMEM, VMEM, VMEM, VMEM],
        out_specs=VMEM,
        scratch_shapes=[
            pltpu.VMEM((rows // CHUNK, 1, CHUNK), I32),
            pltpu.VMEM((owners * rank, capacity), F32),
            pltpu.VMEM((owners * 16, LANES), F32),
        ],
        compiler_params=PARAMS,
        name="pack",
    )(
        jnp.zeros((1,), I32),
        acquired,
        owner.reshape(1, rows),
        slot.reshape(1, rows),
        left_panel.T,
    )
    arrived = lax.all_to_all(packed, "vox", split_axis=0, concat_axis=0, tiled=True)
    core = pl.pallas_call(
        functools.partial(core_kernel, groups),
        out_shape=jax.ShapeDtypeStruct((shares, FINE * rank, width), F32),
        in_specs=[VMEM, VMEM, VMEM],
        out_specs=VMEM,
        scratch_shapes=[
            pltpu.VMEM((FINE * rank, capacity), BF16),
            pltpu.VMEM((FINE * rank, capacity), BF16),
        ],
        compiler_params=PARAMS,
        name="core",
    )(arrived, sampled, right_panel.T)
    share = vox_local // shares
    if shares != 2 or width % LANES:
        total = lax.psum_scatter(core, "echo", scatter_dimension=0)
        total = total.reshape(FINE, rank, width // rank, rank).transpose(2, 0, 1, 3)
        return total.reshape(share, rank * rank).astype(BF16)
    mine = lax.axis_index("echo")
    keep = lax.dynamic_index_in_dim(core, mine, 0, keepdims=False)
    give = lax.dynamic_index_in_dim(core, 1 - mine, 0, keepdims=False).astype(BF16)
    got = lax.ppermute(give, "echo", [(0, 1), (1, 0)])
    return pl.pallas_call(
        functools.partial(finish_kernel, rank),
        out_shape=jax.ShapeDtypeStruct((share, rank * rank), BF16),
        in_specs=[VMEM, VMEM],
        out_specs=VMEM,
        scratch_shapes=[pltpu.VMEM((FINE * rank, LANES), F32)],
        compiler_params=PARAMS,
        name="finish",
    )(keep, got)


def solution(mesh):
    return jax.shard_map(
        on_device,
        mesh=mesh,
        in_specs=(
            P(("vox", "echo"), None),
            P(("vox", "echo"), None),
            P(("vox", "echo"), None),
            P("vox", "echo"),
            P(),
            P("echo", None),
        ),
        out_specs=P(("vox", "echo"), None),
        check_vma=False,
    )
```

```python
import functools

import jax
import jax.numpy as jnp
from jax import lax
from jax.experimental import pallas as pl
from jax.experimental.pallas import tpu as pltpu
from jax.sharding import PartitionSpec as P

LANES = 128
CHUNK = 512
FINE = 16
BF16 = jnp.bfloat16
F32 = jnp.float32
I32 = jnp.int32


def nt_dot(lhs, rhs):
    return lax.dot_general(
        lhs, rhs, (((1,), (1,)), ((), ())), preferred_element_type=F32
    )


def nn_dot(lhs, rhs):
    return lax.dot_general(
        lhs, rhs, (((1,), (0,)), ((), ())), preferred_element_type=F32
    )


def place_rows(owners, me, owner_ref, place_ref):
    rows = owner_ref.shape[1]
    chunks = rows // CHUNK
    owner_range = lax.broadcasted_iota(I32, (owners, CHUNK), 0)
    hots = []
    for j in range(chunks):
        relative = owner_ref[:, j * CHUNK : (j + 1) * CHUNK] ^ me
        hots.append((owner_range == relative).astype(F32))
    hot = jnp.concatenate(hots, axis=0)
    before = lax.broadcasted_iota(I32, (CHUNK, CHUNK), 0) < lax.broadcasted_iota(
        I32, (CHUNK, CHUNK), 1
    )
    prefix = nn_dot(hot.astype(BF16), before.astype(F32).astype(BF16))
    carry = jnp.zeros((owners, 1), F32)
    for j in range(chunks):
        part = prefix[j * owners : (j + 1) * owners]
        place = jnp.sum((part + carry) * hots[j], axis=0, keepdims=True)
        place_ref[j] = place.astype(I32)
        carry = carry + jnp.sum(hots[j], axis=1, keepdims=True)


def put_rows(
    first, capacity, echo_local, me, reduced_ref, owner_ref, slot_ref, place_ref,
    out_refs, feature_ref, id_ref,
):
    rank, rows = reduced_ref.shape
    count = len(out_refs)
    groups = capacity // LANES
    lane_range = lax.broadcasted_iota(I32, (LANES, CHUNK), 0)
    group_range = lax.broadcasted_iota(I32, (8, CHUNK), 0)

    def step(j, _):
        at = pl.multiple_of(j * CHUNK, CHUNK)
        reduced = reduced_ref[:, pl.ds(at, CHUNK)]
        relative = owner_ref[:, pl.ds(at, CHUNK)] ^ me
        slot = slot_ref[:, pl.ds(at, CHUNK)]
        place = place_ref[j]
        group = place // LANES
        lane_hot = (lane_range == place % LANES).astype(F32).astype(BF16)
        group_b = jnp.broadcast_to(group.astype(F32), (LANES, CHUNK)).astype(BF16)
        place_hot = jnp.concatenate(
            [
                jnp.where(group_b == BF16(g), lane_hot, BF16(0))
                for g in range(groups)
            ],
            axis=0,
        )
        here = group_range == group
        voxel = jnp.where(here, (slot // echo_local).astype(F32), 0.0)
        echo = jnp.where(here, (slot % echo_local).astype(F32), 0.0)
        ids = jnp.concatenate([voxel, echo], axis=0).astype(BF16)
        owner_b = jnp.broadcast_to(relative.astype(F32), (rank, CHUNK)).astype(BF16)
        owner_c = owner_b[:16]
        spread = jnp.concatenate(
            [
                jnp.where(owner_b == BF16(first + o), reduced, BF16(0))
                for o in range(count)
            ],
            axis=0,
        )
        spread_ids = jnp.concatenate(
            [
                jnp.where(owner_c == BF16(first + o), ids, BF16(0))
                for o in range(count)
            ],
            axis=0,
        )
        feature = nt_dot(spread, place_hot)
        id_sum = nt_dot(spread_ids, lane_hot)

        @pl.when(j == 0)
        def _():
            feature_ref[...] = feature
            id_ref[...] = id_sum

        @pl.when(j > 0)
        def _():
            feature_ref[...] += feature
            id_ref[...] += id_sum

        return 0

    lax.fori_loop(0, rows // CHUNK, step, 0)
    for o in range(count):
        for g in range(groups):
            out_refs[o][g * rank : (g + 1) * rank, :] = feature_ref[
                o * rank : (o + 1) * rank, g * LANES : (g + 1) * LANES
            ].astype(BF16)
        out_refs[o][groups * rank :, :] = id_ref[o * 16 : (o + 1) * 16, :].astype(BF16)


def far_kernel(
    owners, capacity, echo_local, me_ref, acquired_hbm, owner_hbm, slot_hbm, left_ref,
    reduced_ref, place_ref, *refs,
):
    outs = refs[: owners // 2]
    acquired_ref, owner_ref, slot_ref, feature_ref, id_ref, sems = refs[owners // 2 :]
    copies = [
        pltpu.make_async_copy(a, b, sems.at[i])
        for i, (a, b) in enumerate(
            [(owner_hbm, owner_ref), (slot_hbm, slot_ref), (acquired_hbm, acquired_ref)]
        )
    ]
    for copy in copies:
        copy.start()
    copies[0].wait()
    me = me_ref[0]
    place_rows(owners, me, owner_ref, place_ref)
    copies[1].wait()
    copies[2].wait()
    reduced_ref[...] = nt_dot(left_ref[...], acquired_ref[...]).astype(BF16)
    put_rows(
        owners // 2, capacity, echo_local, me, reduced_ref, owner_ref, slot_ref, place_ref,
        outs, feature_ref, id_ref,
    )


def near_kernel(
    owners, capacity, echo_local, me_ref, owner_ref, slot_ref, reduced_ref, place_ref, *refs
):
    put_rows(
        0, capacity, echo_local, me_ref[0], reduced_ref, owner_ref, slot_ref, place_ref,
        refs[: owners // 2], *refs[owners // 2 :],
    )


def core_kernel(count, halves, more, flip_ref, sampled_ref, right_ref, *refs):
    blocks, refs = refs[:count], refs[count:]
    before = refs[: len(halves)] if more else None
    refs = refs[len(halves) :] if more else refs
    outs, (a_ref, b_ref) = refs[: len(halves)], refs[len(halves) :]
    rank = right_ref.shape[0]
    groups = (blocks[0].shape[0] - 16) // rank
    size = groups * LANES
    half = FINE // 2
    flip = flip_ref[0] * half
    echo_local = sampled_ref.shape[1]
    bits = sampled_ref[0:32, :]
    for b in range(1, sampled_ref.shape[0] // 32):
        bits = bits + (sampled_ref[b * 32 : (b + 1) * 32, :] << b)
    table = jnp.concatenate([right_ref[...], bits.astype(F32).astype(BF16)], axis=0)
    echo_range = lax.broadcasted_iota(I32, (echo_local, LANES), 0).astype(F32).astype(BF16)
    bit_range = lax.broadcasted_iota(I32, (32, LANES), 0)
    for s, block in enumerate(blocks):
        ids = block[groups * rank :, :].astype(F32)
        for g in range(groups):
            feature = block[g * rank : (g + 1) * rank, :]
            voxel = ids[g : g + 1].astype(I32)
            echo = jnp.broadcast_to(ids[8 + g : 9 + g], (echo_local, LANES)).astype(BF16)
            echo_hot = jnp.where(echo == echo_range, BF16(1), BF16(0))
            found = nn_dot(table, echo_hot)
            word = jnp.sum(
                jnp.where(bit_range == voxel % 32, found[rank:], 0.0),
                axis=0, keepdims=True,
            ).astype(I32)
            mask = ((word >> (voxel // 32)) & 1).astype(F32)
            right = (found[:rank] * mask).astype(BF16)
            low = (voxel % FINE).astype(F32)
            high = ((voxel // FINE) ^ flip).astype(F32)
            low = jnp.broadcast_to(low, (rank, LANES)).astype(BF16)
            high = jnp.broadcast_to(high, (rank, LANES)).astype(BF16)
            at = slice(s * size + g * LANES, s * size + (g + 1) * LANES)
            for v in range(FINE):
                a_ref[v * rank : (v + 1) * rank, at] = jnp.where(
                    low == BF16(v), feature, BF16(0)
                )
            for h in halves:
                for v in range(half * h, half * (h + 1)):
                    w = v - half * halves[0]
                    b_ref[w * rank : (w + 1) * rank, at] = jnp.where(
                        high == BF16(v), right, BF16(0)
                    )
    for i in range(len(halves)):
        total = nt_dot(a_ref[...], b_ref[i * half * rank : (i + 1) * half * rank, :])
        if more:
            total = total + before[i][...]
        outs[i][...] = total.astype(outs[i].dtype)


def finish_kernel(rank, keep_ref, got_ref, out_ref, sum_ref):
    tiles = keep_ref.shape[1] // LANES
    per = LANES // rank
    block = lax.broadcasted_iota(I32, (FINE, LANES), 1) // rank
    for t in range(tiles):
        sum_ref[...] = (
            keep_ref[:, t * LANES : (t + 1) * LANES]
            + got_ref[:, t * LANES : (t + 1) * LANES].astype(F32)
        )
        for q in range(rank // per):
            rows = [
                sum_ref[pl.ds(q * per + i, FINE, stride=rank), :] for i in range(per)
            ]
            for k in range(per):
                made = None
                for i in range(per):
                    turn = (i - k) % per * rank
                    moved = pltpu.roll(rows[i], turn, 1) if turn else rows[i]
                    made = moved if made is None else jnp.where(block == i, moved, made)
                v = t * per + k
                out_ref[v * FINE : (v + 1) * FINE, q * LANES : (q + 1) * LANES] = (
                    made.astype(BF16)
                )


VMEM = pl.BlockSpec(memory_space=pltpu.VMEM)
SMEM = pl.BlockSpec(memory_space=pltpu.SMEM)
ANY = pl.BlockSpec(memory_space=pl.ANY)
PARAMS = pltpu.CompilerParams(vmem_limit_bytes=40 * 2**20)


def core_call(blocks, flip, sampled, right, halves=(0, 1), before=(), kinds=None):
    rank = right.shape[0]
    groups = (blocks[0].shape[0] - 16) // rank
    rows = len(blocks) * groups * LANES
    wide, narrow = FINE * rank, FINE * rank // 2
    first = 3 + len(blocks)
    kinds = kinds or [F32] * len(halves)
    return pl.pallas_call(
        functools.partial(core_kernel, len(blocks), halves, bool(before)),
        out_shape=[jax.ShapeDtypeStruct((wide, narrow), kind) for kind in kinds],
        in_specs=[SMEM] + [VMEM] * (2 + len(blocks) + len(before)),
        out_specs=[VMEM] * len(halves),
        scratch_shapes=[
            pltpu.VMEM((wide, rows), BF16),
            pltpu.VMEM((narrow * len(halves), rows), BF16),
        ],
        input_output_aliases={
            first + i: i for i in range(len(before)) if kinds[i] == F32
        },
        compiler_params=PARAMS,
        cost_estimate=pl.CostEstimate(
            flops=2 * rows * wide * narrow * len(halves),
            bytes_accessed=rows * 68 + 4 * wide * narrow * len(halves),
            transcendentals=0,
        ),
        name="core",
    )(flip, sampled, right, *blocks, *before)


def on_device(acquired, owner, slot, sampled, left_panel, right_panel):
    owners = lax.axis_size("vox")
    shares = lax.axis_size("echo")
    rows = acquired.shape[0]
    capacity = 4 * rows // owners
    groups = capacity // LANES
    vox_local, echo_local = sampled.shape
    rank = left_panel.shape[1]
    depth = groups * rank + 16
    half = owners // 2
    me = lax.axis_index("vox").reshape(1)
    mine = lax.axis_index("echo")
    owner, slot = owner.reshape(1, rows), slot.reshape(1, rows)
    left, right = left_panel.T, right_panel.T
    block = jax.ShapeDtypeStruct((depth, LANES), BF16)
    sums = [
        pltpu.VMEM((half * rank, capacity), F32),
        pltpu.VMEM((half * 16, LANES), F32),
    ]
    cost = pl.CostEstimate(
        flops=2 * rows * capacity * half * rank,
        bytes_accessed=4 * rows * 128,
        transcendentals=0,
    )
    reduced, place, *far = pl.pallas_call(
        functools.partial(far_kernel, owners, capacity, echo_local),
        out_shape=[
            jax.ShapeDtypeStruct((rank, rows), BF16),
            jax.ShapeDtypeStruct((rows // CHUNK, 1, CHUNK), I32),
        ]
        + [block] * half,
        in_specs=[SMEM, ANY, ANY, ANY, VMEM],
        out_specs=[VMEM] * (2 + half),
        scratch_shapes=[
            pltpu.VMEM(acquired.shape, BF16),
            pltpu.VMEM(owner.shape, I32),
            pltpu.VMEM(slot.shape, I32),
            *sums,
            pltpu.SemaphoreType.DMA((3,)),
        ],
        compiler_params=PARAMS,
        cost_estimate=cost,
        name="far",
    )(me, acquired, owner, slot, left)
    near = pl.pallas_call(
        functools.partial(near_kernel, owners, capacity, echo_local),
        out_shape=[block] * half,
        in_specs=[SMEM] + [VMEM] * 4,
        out_specs=[VMEM] * half,
        scratch_shapes=sums,
        compiler_params=PARAMS,
        cost_estimate=cost,
        name="near",
    )(me, owner, slot, reduced, place)

    def sent(array, mask):
        return lax.ppermute(array, "vox", [(i, i ^ mask) for i in range(owners)])

    order = [*range(half, owners, 2), *range(half + 1, owners, 2)]
    arrived = {m: sent(far[m - half], m) for m in order}
    arrived.update({m: sent(near[m], m) if m else near[0] for m in range(half)})
    two = shares == 2
    flip = ((1 - mine) if two else jnp.zeros((), I32)).astype(I32).reshape(1)
    run = functools.partial(core_call, flip=flip, sampled=sampled, right=right)
    total = run([arrived[m] for m in range(half)])
    late = order[-2:]
    done = order[:-2]
    for i in range(0, len(done), 4):
        total = run([arrived[m] for m in done[i : i + 4]], before=total)
    last = [arrived[m] for m in late]
    share = vox_local // shares
    if not two:
        both = jnp.concatenate(run(last, before=total), axis=1)
        both = both.reshape(FINE * rank, shares, FINE * rank // shares)
        both = lax.psum_scatter(both, "echo", scatter_dimension=1)
        both = both.reshape(FINE, rank, FINE // shares, rank).transpose(2, 0, 1, 3)
        return both.reshape(share, rank * rank).astype(BF16)
    (give,) = run(last, halves=(0,), before=total[:1], kinds=[BF16])
    got = lax.ppermute(give, "echo", [(0, 1), (1, 0)])
    (keep,) = run(last, halves=(1,), before=total[1:])
    return pl.pallas_call(
        functools.partial(finish_kernel, rank),
        out_shape=jax.ShapeDtypeStruct((share, rank * rank), BF16),
        in_specs=[VMEM, VMEM],
        out_specs=VMEM,
        scratch_shapes=[pltpu.VMEM((FINE * rank, LANES), F32)],
        compiler_params=PARAMS,
        name="finish",
    )(keep, got)


def solution(mesh):
    return jax.shard_map(
        on_device,
        mesh=mesh,
        in_specs=(
            P(("vox", "echo"), None),
            P(("vox", "echo"), None),
            P(("vox", "echo"), None),
            P("vox", "echo"),
            P(),
            P("echo", None),
        ),
        out_specs=P(("vox", "echo"), None),
        check_vma=False,
    )
```

```python
import functools

import jax
import jax.numpy as jnp
from jax import lax
from jax.experimental import pallas as pl
from jax.experimental.pallas import tpu as pltpu
from jax.sharding import PartitionSpec as P

LANES = 128
CHUNK = 512
STEP = 1024
FINE = 16
BF16 = jnp.bfloat16
F32 = jnp.float32
I32 = jnp.int32


def nt_dot(lhs, rhs):
    return lax.dot_general(
        lhs, rhs, (((1,), (1,)), ((), ())), preferred_element_type=F32
    )


def nn_dot(lhs, rhs):
    return lax.dot_general(
        lhs, rhs, (((1,), (0,)), ((), ())), preferred_element_type=F32
    )


def place_rows(owners, me, owner_ref, place_ref):
    rows = owner_ref.shape[1]
    chunks = rows // CHUNK
    owner_range = lax.broadcasted_iota(I32, (owners, CHUNK), 0)
    hots = []
    for j in range(chunks):
        relative = owner_ref[:, j * CHUNK : (j + 1) * CHUNK] ^ me
        hots.append((owner_range == relative).astype(F32))
    hot = jnp.concatenate(hots, axis=0)
    before = lax.broadcasted_iota(I32, (CHUNK, CHUNK), 0) < lax.broadcasted_iota(
        I32, (CHUNK, CHUNK), 1
    )
    prefix = nn_dot(hot.astype(BF16), before.astype(F32).astype(BF16))
    carry = jnp.zeros((owners, 1), F32)
    for j in range(chunks):
        part = prefix[j * owners : (j + 1) * owners]
        place = jnp.sum((part + carry) * hots[j], axis=0, keepdims=True)
        place_ref[j] = place.astype(I32)
        carry = carry + jnp.sum(hots[j], axis=1, keepdims=True)


def put_rows(
    first, capacity, echo_local, me, reduced_ref, owner_ref, slot_ref, place_ref,
    out_refs, spread_ref, hot_ref, ids_ref,
):
    rank, rows = reduced_ref.shape
    count = len(out_refs)
    groups = capacity // LANES
    lane_range = lax.broadcasted_iota(I32, (LANES, STEP), 0).astype(F32).astype(BF16)
    group_range = lax.broadcasted_iota(I32, (8, STEP), 0)

    def level(row, height):
        return jnp.broadcast_to(row.astype(F32), (height, STEP)).astype(BF16)

    for j in range(rows // STEP):
        at = slice(j * STEP, (j + 1) * STEP)
        reduced = reduced_ref[:, at]
        relative = owner_ref[:, at] ^ me
        slot = slot_ref[:, at]
        place = jnp.concatenate(
            [place_ref[j * (STEP // CHUNK) + i] for i in range(STEP // CHUNK)], axis=1
        )
        group = place // LANES
        lane = level(place % LANES, LANES)
        lane_hot = jnp.where(lane_range == lane, BF16(1), BF16(0))
        group_b = level(group, LANES)
        for g in range(groups):
            hot_ref[g * LANES : (g + 1) * LANES, at] = jnp.where(
                group_b == BF16(g), lane_hot, BF16(0)
            )
        here = group_range == group
        voxel = jnp.where(here, (slot // echo_local).astype(F32), 0.0)
        echo = jnp.where(here, (slot % echo_local).astype(F32), 0.0)
        ids = jnp.concatenate([voxel, echo], axis=0).astype(BF16)
        owner_b = level(relative, rank)
        owner_c = level(relative, 16)
        for o in range(count):
            spread_ref[o * rank : (o + 1) * rank, at] = jnp.where(
                owner_b == BF16(first + o), reduced, BF16(0)
            )
        spread_ids = jnp.concatenate(
            [
                jnp.where(owner_c == BF16(first + o), ids, BF16(0))
                for o in range(count)
            ],
            axis=0,
        )
        part = nt_dot(spread_ids, lane_hot)
        ids_ref[...] = part if j == 0 else ids_ref[...] + part
    for o in range(count):
        out_refs[o][groups * rank :, :] = ids_ref[o * 16 : (o + 1) * 16, :].astype(BF16)
    wide = 2 * LANES
    for g in range(0, groups, 2):
        made = nt_dot(spread_ref[...], hot_ref[g * LANES : g * LANES + wide, :]).astype(BF16)
        for o in range(count):
            for i in range(2):
                out_refs[o][(g + i) * rank : (g + i + 1) * rank, :] = made[
                    o * rank : (o + 1) * rank, i * LANES : (i + 1) * LANES
                ]


def far_kernel(
    owners, capacity, echo_local, me_ref, acquired_hbm, owner_hbm, slot_hbm, left_hbm,
    reduced_ref, place_ref, owner_ref, slot_ref, *refs,
):
    outs = refs[: owners // 2]
    acquired_ref, left_ref, spread_ref, hot_ref, ids_ref, sems = refs[owners // 2 :]
    copies = [
        pltpu.make_async_copy(a, b, sems.at[i])
        for i, (a, b) in enumerate(
            [
                (owner_hbm, owner_ref),
                (slot_hbm, slot_ref),
                (acquired_hbm, acquired_ref),
                (left_hbm, left_ref),
            ]
        )
    ]
    for copy in copies:
        copy.start()
    copies[0].wait()
    me = me_ref[0]
    place_rows(owners, me, owner_ref, place_ref)
    for copy in copies[1:]:
        copy.wait()
    reduced_ref[...] = nt_dot(left_ref[...], acquired_ref[...]).astype(BF16)
    put_rows(
        owners // 2, capacity, echo_local, me, reduced_ref, owner_ref, slot_ref, place_ref,
        outs, spread_ref, hot_ref, ids_ref,
    )


def near_kernel(
    owners, capacity, echo_local, me_ref, owner_ref, slot_ref, reduced_ref, place_ref, *refs
):
    put_rows(
        0, capacity, echo_local, me_ref[0], reduced_ref, owner_ref, slot_ref, place_ref,
        refs[: owners // 2], *refs[owners // 2 :],
    )


def core_kernel(count, halves, more, flip_ref, sampled_ref, right_ref, *refs):
    blocks, refs = refs[:count], refs[count:]
    before = refs[: len(halves)] if more else None
    refs = refs[len(halves) :] if more else refs
    outs, (a_ref, b_ref) = refs[: len(halves)], refs[len(halves) :]
    rank = right_ref.shape[0]
    groups = (blocks[0].shape[0] - 16) // rank
    size = groups * LANES
    half = FINE // 2
    flip = flip_ref[0] * half
    echo_local = sampled_ref.shape[1]
    bits = sampled_ref[0:32, :]
    for b in range(1, sampled_ref.shape[0] // 32):
        bits = bits + (sampled_ref[b * 32 : (b + 1) * 32, :] << b)
    table = jnp.concatenate([right_ref[...], bits.astype(F32).astype(BF16)], axis=0)
    echo_range = lax.broadcasted_iota(I32, (echo_local, LANES), 0).astype(F32).astype(BF16)
    bit_range = lax.broadcasted_iota(I32, (32, LANES), 0)
    for s, block in enumerate(blocks):
        ids = block[groups * rank :, :].astype(F32)
        for g in range(groups):
            feature = block[g * rank : (g + 1) * rank, :]
            voxel = ids[g : g + 1].astype(I32)
            echo = jnp.broadcast_to(ids[8 + g : 9 + g], (echo_local, LANES)).astype(BF16)
            echo_hot = jnp.where(echo == echo_range, BF16(1), BF16(0))
            found = nn_dot(table, echo_hot)
            word = jnp.sum(
                jnp.where(bit_range == voxel % 32, found[rank:], 0.0),
                axis=0, keepdims=True,
            ).astype(I32)
            mask = ((word >> (voxel // 32)) & 1).astype(F32)
            right = (found[:rank] * mask).astype(BF16)
            low = (voxel % FINE).astype(F32)
            high = ((voxel // FINE) ^ flip).astype(F32)
            low = jnp.broadcast_to(low, (rank, LANES)).astype(BF16)
            high = jnp.broadcast_to(high, (rank, LANES)).astype(BF16)
            at = slice(s * size + g * LANES, s * size + (g + 1) * LANES)
            for v in range(FINE):
                a_ref[v * rank : (v + 1) * rank, at] = jnp.where(
                    low == BF16(v), feature, BF16(0)
                )
            for h in halves:
                for v in range(half * h, half * (h + 1)):
                    w = v - half * halves[0]
                    b_ref[w * rank : (w + 1) * rank, at] = jnp.where(
                        high == BF16(v), right, BF16(0)
                    )
    for i in range(len(halves)):
        total = nt_dot(a_ref[...], b_ref[i * half * rank : (i + 1) * half * rank, :])
        if more:
            total = total + before[i][...]
        outs[i][...] = total.astype(outs[i].dtype)


def finish_kernel(rank, keep_ref, got_ref, out_ref, sum_ref):
    tiles = keep_ref.shape[1] // LANES
    per = LANES // rank
    block = lax.broadcasted_iota(I32, (FINE, LANES), 1) // rank
    for t in range(tiles):
        sum_ref[...] = (
            keep_ref[:, t * LANES : (t + 1) * LANES]
            + got_ref[:, t * LANES : (t + 1) * LANES].astype(F32)
        )
        for q in range(rank // per):
            rows = [
                sum_ref[pl.ds(q * per + i, FINE, stride=rank), :] for i in range(per)
            ]
            for k in range(per):
                made = None
                for i in range(per):
                    turn = (i - k) % per * rank
                    moved = pltpu.roll(rows[i], turn, 1) if turn else rows[i]
                    made = moved if made is None else jnp.where(block == i, moved, made)
                v = t * per + k
                out_ref[v * FINE : (v + 1) * FINE, q * LANES : (q + 1) * LANES] = (
                    made.astype(BF16)
                )


VMEM = pl.BlockSpec(memory_space=pltpu.VMEM)
SMEM = pl.BlockSpec(memory_space=pltpu.SMEM)
HBM = pl.BlockSpec(memory_space=pltpu.HBM)
PARAMS = pltpu.CompilerParams(vmem_limit_bytes=40 * 2**20)


def core_call(blocks, flip, sampled, right, halves=(0, 1), before=(), kinds=None):
    rank = right.shape[0]
    groups = (blocks[0].shape[0] - 16) // rank
    rows = len(blocks) * groups * LANES
    wide, narrow = FINE * rank, FINE * rank // 2
    first = 3 + len(blocks)
    kinds = kinds or [F32] * len(halves)
    return pl.pallas_call(
        functools.partial(core_kernel, len(blocks), halves, bool(before)),
        out_shape=[jax.ShapeDtypeStruct((wide, narrow), kind) for kind in kinds],
        in_specs=[SMEM] + [VMEM] * (2 + len(blocks) + len(before)),
        out_specs=[VMEM] * len(halves),
        scratch_shapes=[
            pltpu.VMEM((wide, rows), BF16),
            pltpu.VMEM((narrow * len(halves), rows), BF16),
        ],
        input_output_aliases={
            first + i: i for i in range(len(before)) if kinds[i] == F32
        },
        compiler_params=PARAMS,
        cost_estimate=pl.CostEstimate(
            flops=2 * rows * wide * narrow * len(halves),
            bytes_accessed=rows * 68 + 4 * wide * narrow * len(halves),
            transcendentals=0,
        ),
        name="core",
    )(flip, sampled, right, *blocks, *before)


def on_device(acquired, owner, slot, sampled, left_panel, right_panel):
    owners = lax.axis_size("vox")
    shares = lax.axis_size("echo")
    rows = acquired.shape[0]
    capacity = 4 * rows // owners
    groups = capacity // LANES
    vox_local, echo_local = sampled.shape
    rank = left_panel.shape[1]
    depth = groups * rank + 16
    half = owners // 2
    me = lax.axis_index("vox").reshape(1)
    mine = lax.axis_index("echo")
    owner, slot = owner.reshape(1, rows), slot.reshape(1, rows)
    left, right = left_panel.T, right_panel.T
    block = jax.ShapeDtypeStruct((depth, LANES), BF16)
    sums = [
        pltpu.VMEM((half * rank, rows), BF16),
        pltpu.VMEM((capacity, rows), BF16),
        pltpu.VMEM((half * 16, LANES), F32),
    ]
    cost = pl.CostEstimate(
        flops=2 * rows * capacity * half * rank,
        bytes_accessed=4 * rows * 128,
        transcendentals=0,
    )
    reduced, place, owner, slot, *far = pl.pallas_call(
        functools.partial(far_kernel, owners, capacity, echo_local),
        out_shape=[
            jax.ShapeDtypeStruct((rank, rows), BF16),
            jax.ShapeDtypeStruct((rows // CHUNK, 1, CHUNK), I32),
            jax.ShapeDtypeStruct(owner.shape, I32),
            jax.ShapeDtypeStruct(slot.shape, I32),
        ]
        + [block] * half,
        in_specs=[SMEM, HBM, HBM, HBM, HBM],
        out_specs=[VMEM] * (4 + half),
        scratch_shapes=[
            pltpu.VMEM(acquired.shape, BF16),
            pltpu.VMEM(left.shape, BF16),
            *sums,
            pltpu.SemaphoreType.DMA((4,)),
        ],
        compiler_params=PARAMS,
        cost_estimate=cost,
        name="far",
    )(me, *[pltpu.with_memory_space_constraint(x, pltpu.HBM) for x in (acquired, owner, slot, left)])
    near = pl.pallas_call(
        functools.partial(near_kernel, owners, capacity, echo_local),
        out_shape=[block] * half,
        in_specs=[SMEM] + [VMEM] * 4,
        out_specs=[VMEM] * half,
        scratch_shapes=sums,
        compiler_params=PARAMS,
        cost_estimate=cost,
        name="near",
    )(me, owner, slot, reduced, place)

    def sent(array, mask):
        return lax.ppermute(array, "vox", [(i, i ^ mask) for i in range(owners)])

    order = [*range(half, owners, 2), *range(half + 1, owners, 2)]
    arrived = {m: sent(far[m - half], m) for m in order}
    arrived.update({m: sent(near[m], m) if m else near[0] for m in range(half)})
    two = shares == 2
    flip = ((1 - mine) if two else jnp.zeros((), I32)).astype(I32).reshape(1)
    run = functools.partial(core_call, flip=flip, sampled=sampled, right=right)
    total = run([arrived[m] for m in range(half)])
    late = order[-2:]
    done = order[:-2]
    for i in range(0, len(done), 4):
        total = run([arrived[m] for m in done[i : i + 4]], before=total)
    last = [arrived[m] for m in late]
    share = vox_local // shares
    if not two:
        both = jnp.concatenate(run(last, before=total), axis=1)
        both = both.reshape(FINE * rank, shares, FINE * rank // shares)
        both = lax.psum_scatter(both, "echo", scatter_dimension=1)
        both = both.reshape(FINE, rank, FINE // shares, rank).transpose(2, 0, 1, 3)
        return both.reshape(share, rank * rank).astype(BF16)
    (give,) = run(last, halves=(0,), before=total[:1], kinds=[BF16])
    got = lax.ppermute(give, "echo", [(0, 1), (1, 0)])
    (keep,) = run(last, halves=(1,), before=total[1:])
    return pl.pallas_call(
        functools.partial(finish_kernel, rank),
        out_shape=jax.ShapeDtypeStruct((share, rank * rank), BF16),
        in_specs=[VMEM, VMEM],
        out_specs=VMEM,
        scratch_shapes=[pltpu.VMEM((FINE * rank, LANES), F32)],
        compiler_params=PARAMS,
        name="finish",
    )(keep, got)


def solution(mesh):
    return jax.shard_map(
        on_device,
        mesh=mesh,
        in_specs=(
            P(("vox", "echo"), None),
            P(("vox", "echo"), None),
            P(("vox", "echo"), None),
            P("vox", "echo"),
            P(),
            P("echo", None),
        ),
        out_specs=P(("vox", "echo"), None),
        check_vma=False,
    )
```

```python
import functools

import jax
import jax.numpy as jnp
from jax import lax
from jax.experimental import pallas as pl
from jax.experimental.pallas import tpu as pltpu
from jax.sharding import PartitionSpec as P

LANES = 128
CHUNK = 512
STEP = 1024
FINE = 16
BF16 = jnp.bfloat16
F32 = jnp.float32
I32 = jnp.int32


def nt_dot(lhs, rhs):
    return lax.dot_general(
        lhs, rhs, (((1,), (1,)), ((), ())), preferred_element_type=F32
    )


def nn_dot(lhs, rhs):
    return lax.dot_general(
        lhs, rhs, (((1,), (0,)), ((), ())), preferred_element_type=F32
    )


def chip_masks(owners):
    chips = owners // 4
    far = range(chips, 2 * chips)
    return list(far[0::2]), list(far[1::2]), list(range(1, chips))


def place_rows(owners, me, owner_ref, place_ref):
    rows = owner_ref.shape[1]
    chunks = rows // CHUNK
    owner_range = lax.broadcasted_iota(I32, (owners, CHUNK), 0)
    hots = []
    for j in range(chunks):
        relative = owner_ref[:, j * CHUNK : (j + 1) * CHUNK] ^ me
        hots.append((owner_range == relative).astype(F32))
    hot = jnp.concatenate(hots, axis=0)
    before = lax.broadcasted_iota(I32, (CHUNK, CHUNK), 0) < lax.broadcasted_iota(
        I32, (CHUNK, CHUNK), 1
    )
    prefix = nn_dot(hot.astype(BF16), before.astype(F32).astype(BF16))
    carry = jnp.zeros((owners, 1), F32)
    for j in range(chunks):
        part = prefix[j * owners : (j + 1) * owners]
        place = jnp.sum((part + carry) * hots[j], axis=0, keepdims=True)
        place_ref[j] = place.astype(I32)
        carry = carry + jnp.sum(hots[j], axis=1, keepdims=True)


def put_rows(
    wanted, capacity, echo_local, me, reduced_ref, owner_ref, slot_ref, place_ref,
    slots, spread_ref, hot_ref, ids_ref,
):
    rank, rows = reduced_ref.shape
    count = len(slots)
    groups = capacity // LANES
    lane_range = lax.broadcasted_iota(I32, (LANES, STEP), 0).astype(F32).astype(BF16)
    group_range = lax.broadcasted_iota(I32, (8, STEP), 0)

    def level(row, height):
        return jnp.broadcast_to(row.astype(F32), (height, STEP)).astype(BF16)

    for j in range(rows // STEP):
        at = slice(j * STEP, (j + 1) * STEP)
        reduced = reduced_ref[:, at]
        relative = owner_ref[:, at] ^ me
        slot = slot_ref[:, at]
        place = jnp.concatenate(
            [place_ref[j * (STEP // CHUNK) + i] for i in range(STEP // CHUNK)], axis=1
        )
        group = place // LANES
        lane = level(place % LANES, LANES)
        lane_hot = jnp.where(lane_range == lane, BF16(1), BF16(0))
        group_b = level(group, LANES)
        for g in range(groups):
            hot_ref[g * LANES : (g + 1) * LANES, at] = jnp.where(
                group_b == BF16(g), lane_hot, BF16(0)
            )
        here = group_range == group
        voxel = jnp.where(here, (slot // echo_local).astype(F32), 0.0)
        echo = jnp.where(here, (slot % echo_local).astype(F32), 0.0)
        ids = jnp.concatenate([voxel, echo], axis=0).astype(BF16)
        owner_b = level(relative, rank)
        owner_c = level(relative, 16)
        for o in range(count):
            spread_ref[o * rank : (o + 1) * rank, at] = jnp.where(
                owner_b == BF16(wanted[o]), reduced, BF16(0)
            )
        spread_ids = jnp.concatenate(
            [
                jnp.where(owner_c == BF16(wanted[o]), ids, BF16(0))
                for o in range(count)
            ],
            axis=0,
        )
        part = nt_dot(spread_ids, lane_hot)
        ids_ref[...] = part if j == 0 else ids_ref[...] + part
    for o, (out_ref, base) in enumerate(slots):
        base += groups * rank
        out_ref[base : base + 16, :] = ids_ref[o * 16 : (o + 1) * 16, :].astype(BF16)
    wide = 2 * LANES
    for g in range(0, groups, 2):
        made = nt_dot(spread_ref[...], hot_ref[g * LANES : g * LANES + wide, :]).astype(BF16)
        for o, (out_ref, base) in enumerate(slots):
            for i in range(2):
                at = base + (g + i) * rank
                out_ref[at : at + rank, :] = made[
                    o * rank : (o + 1) * rank, i * LANES : (i + 1) * LANES
                ]


def early_kernel(
    owners, capacity, echo_local, me_ref, acquired_hbm, owner_hbm, slot_hbm, left_hbm,
    reduced_ref, place_ref, owner_ref, slot_ref, *refs,
):
    chips = owners // 4
    pairs, refs = refs[: chips // 2], refs[chips // 2 :]
    apart_ref, acquired_ref, left_ref, spread_ref, hot_ref, ids_ref, sems = refs
    depth = pairs[0].shape[0] // 2
    copies = [
        pltpu.make_async_copy(a, b, sems.at[i])
        for i, (a, b) in enumerate(
            [
                (owner_hbm, owner_ref),
                (slot_hbm, slot_ref),
                (acquired_hbm, acquired_ref),
                (left_hbm, left_ref),
            ]
        )
    ]
    for copy in copies:
        copy.start()
    copies[0].wait()
    me = me_ref[0]
    place_rows(owners, me, owner_ref, place_ref)
    for copy in copies[1:]:
        copy.wait()
    reduced_ref[...] = nt_dot(left_ref[...], acquired_ref[...]).astype(BF16)
    early, late, close = chip_masks(owners)
    wanted, slots = [], []
    for m, pair in zip(early, pairs):
        wanted += [2 * m, 2 * m + 1]
        slots += [(pair, 0), (pair, depth)]
    for i, m in enumerate([0, *late, *close]):
        wanted.append(2 * m + 1)
        slots.append((apart_ref, i * depth))
    put_rows(
        wanted, capacity, echo_local, me, reduced_ref, owner_ref, slot_ref, place_ref,
        slots, spread_ref, hot_ref, ids_ref,
    )


def rest_kernel(
    owners, capacity, echo_local, me_ref, owner_ref, slot_ref, reduced_ref, place_ref,
    other_ref, own_ref, *refs,
):
    _, late, close = chip_masks(owners)
    masks = [*late, *close]
    joined, scratch = refs[: len(masks)], refs[len(masks) :]
    depth = own_ref.shape[0]
    for i, ref in enumerate(joined):
        ref[depth:, :] = other_ref[(i + 1) * depth : (i + 2) * depth, :]
    put_rows(
        [0, *[2 * m for m in masks]], capacity, echo_local, me_ref[0],
        reduced_ref, owner_ref, slot_ref, place_ref,
        [(own_ref, 0), *[(ref, 0) for ref in joined]], *scratch,
    )


def core_kernel(
    plan, depth, halves, more, flip_ref, sampled_ref, right_ref, *refs
):
    arrays, refs = refs[: len(plan)], refs[len(plan) :]
    blocks = [(r, i * depth) for r, p in zip(arrays, plan) for i in p[0]]
    onward = [(r, i * depth) for r, p in zip(arrays, plan) for i in p[1]]
    before = refs[: len(halves)] if more else None
    refs = refs[len(halves) :] if more else refs
    outs, refs = refs[: len(halves)], refs[len(halves) :]
    if onward:
        for out_ref, (ref, base) in zip(refs, onward):
            out_ref[...] = ref[base : base + depth, :]
        refs = refs[len(onward) :]
    a_ref, b_ref = refs
    rank = right_ref.shape[0]
    groups = (depth - 16) // rank
    size = groups * LANES
    half = FINE // 2
    flip = flip_ref[0] * half
    echo_local = sampled_ref.shape[1]
    bits = sampled_ref[0:32, :]
    for b in range(1, sampled_ref.shape[0] // 32):
        bits = bits + (sampled_ref[b * 32 : (b + 1) * 32, :] << b)
    table = jnp.concatenate([right_ref[...], bits.astype(F32).astype(BF16)], axis=0)
    echo_range = lax.broadcasted_iota(I32, (echo_local, LANES), 0).astype(F32).astype(BF16)
    bit_range = lax.broadcasted_iota(I32, (32, LANES), 0)
    for s, (ref, base) in enumerate(blocks):
        ids = ref[base + groups * rank : base + depth, :].astype(F32)
        for g in range(groups):
            feature = ref[base + g * rank : base + (g + 1) * rank, :]
            voxel = ids[g : g + 1].astype(I32)
            echo = jnp.broadcast_to(ids[8 + g : 9 + g], (echo_local, LANES)).astype(BF16)
            echo_hot = jnp.where(echo == echo_range, BF16(1), BF16(0))
            found = nn_dot(table, echo_hot)
            word = jnp.sum(
                jnp.where(bit_range == voxel % 32, found[rank:], 0.0),
                axis=0, keepdims=True,
            ).astype(I32)
            mask = ((word >> (voxel // 32)) & 1).astype(F32)
            right = (found[:rank] * mask).astype(BF16)
            low = (voxel % FINE).astype(F32)
            high = ((voxel // FINE) ^ flip).astype(F32)
            low = jnp.broadcast_to(low, (rank, LANES)).astype(BF16)
            high = jnp.broadcast_to(high, (rank, LANES)).astype(BF16)
            at = slice(s * size + g * LANES, s * size + (g + 1) * LANES)
            for v in range(FINE):
                a_ref[v * rank : (v + 1) * rank, at] = jnp.where(
                    low == BF16(v), feature, BF16(0)
                )
            for h in halves:
                for v in range(half * h, half * (h + 1)):
                    w = v - half * halves[0]
                    b_ref[w * rank : (w + 1) * rank, at] = jnp.where(
                        high == BF16(v), right, BF16(0)
                    )
    for i in range(len(halves)):
        total = nt_dot(a_ref[...], b_ref[i * half * rank : (i + 1) * half * rank, :])
        if more:
            total = total + before[i][...]
        outs[i][...] = total.astype(outs[i].dtype)


def finish_kernel(rank, keep_ref, got_ref, out_ref, sum_ref):
    tiles = keep_ref.shape[1] // LANES
    per = LANES // rank
    block = lax.broadcasted_iota(I32, (FINE, LANES), 1) // rank
    for t in range(tiles):
        sum_ref[...] = (
            keep_ref[:, t * LANES : (t + 1) * LANES]
            + got_ref[:, t * LANES : (t + 1) * LANES].astype(F32)
        )
        for q in range(rank // per):
            rows = [
                sum_ref[pl.ds(q * per + i, FINE, stride=rank), :] for i in range(per)
            ]
            for k in range(per):
                made = None
                for i in range(per):
                    turn = (i - k) % per * rank
                    moved = pltpu.roll(rows[i], turn, 1) if turn else rows[i]
                    made = moved if made is None else jnp.where(block == i, moved, made)
                v = t * per + k
                out_ref[v * FINE : (v + 1) * FINE, q * LANES : (q + 1) * LANES] = (
                    made.astype(BF16)
                )


VMEM = pl.BlockSpec(memory_space=pltpu.VMEM)
SMEM = pl.BlockSpec(memory_space=pltpu.SMEM)
HBM = pl.BlockSpec(memory_space=pltpu.HBM)
PARAMS = pltpu.CompilerParams(vmem_limit_bytes=40 * 2**20)


def core_call(
    arrays, plan, depth, flip, sampled, right, halves=(0, 1), before=(), kinds=None
):
    rank = right.shape[0]
    groups = (depth - 16) // rank
    count = sum(len(p[0]) for p in plan)
    onward = sum(len(p[1]) for p in plan)
    rows = count * groups * LANES
    wide, narrow = FINE * rank, FINE * rank // 2
    first = 3 + len(arrays)
    kinds = kinds or [F32] * len(halves)
    shapes = [jax.ShapeDtypeStruct((wide, narrow), kind) for kind in kinds]
    shapes += [jax.ShapeDtypeStruct((depth, LANES), BF16)] * onward
    return pl.pallas_call(
        functools.partial(core_kernel, plan, depth, halves, bool(before)),
        out_shape=shapes,
        in_specs=[SMEM] + [VMEM] * (2 + len(arrays) + len(before)),
        out_specs=[VMEM] * len(shapes),
        scratch_shapes=[
            pltpu.VMEM((wide, rows), BF16),
            pltpu.VMEM((narrow * len(halves), rows), BF16),
        ],
        input_output_aliases={
            first + i: i for i in range(len(before)) if kinds[i] == F32
        },
        compiler_params=PARAMS,
        cost_estimate=pl.CostEstimate(flops=1, bytes_accessed=1, transcendentals=0),
        name="core",
    )(flip, sampled, right, *arrays, *before)


def on_device(acquired, owner, slot, sampled, left_panel, right_panel):
    owners = lax.axis_size("vox")
    shares = lax.axis_size("echo")
    rows = acquired.shape[0]
    capacity = 4 * rows // owners
    groups = capacity // LANES
    vox_local, echo_local = sampled.shape
    rank = left_panel.shape[1]
    depth = groups * rank + 16
    early, late, close = chip_masks(owners)
    me = lax.axis_index("vox").reshape(1)
    mine = lax.axis_index("echo")
    owner, slot = owner.reshape(1, rows), slot.reshape(1, rows)
    left, right = left_panel.T, right_panel.T

    def blocks(n):
        return jax.ShapeDtypeStruct((n * depth, LANES), BF16)

    def sent(array, mask):
        return lax.ppermute(array, "vox", [(i, i ^ mask) for i in range(owners)])

    def scratch(n):
        return [
            pltpu.VMEM((n * rank, rows), BF16),
            pltpu.VMEM((capacity, rows), BF16),
            pltpu.VMEM((n * 16, LANES), F32),
        ]

    cost = pl.CostEstimate(
        flops=rows * capacity * owners * rank,
        bytes_accessed=4 * rows * 128,
        transcendentals=0,
    )
    across = 1 + len(late) + len(close)
    shapes = [
        jax.ShapeDtypeStruct((rank, rows), BF16),
        jax.ShapeDtypeStruct((rows // CHUNK, 1, CHUNK), I32),
        jax.ShapeDtypeStruct(owner.shape, I32),
        jax.ShapeDtypeStruct(slot.shape, I32),
        *[blocks(2)] * len(early),
        blocks(across),
    ]
    hbm = [
        pltpu.with_memory_space_constraint(x, pltpu.HBM)
        for x in (acquired, owner, slot, left)
    ]
    reduced, place, owner, slot, *pairs, apart = pl.pallas_call(
        functools.partial(early_kernel, owners, capacity, echo_local),
        out_shape=shapes,
        in_specs=[SMEM, HBM, HBM, HBM, HBM],
        out_specs=[VMEM] * len(shapes),
        scratch_shapes=[
            pltpu.VMEM(acquired.shape, BF16),
            pltpu.VMEM(left.shape, BF16),
            *scratch(2 * len(early) + across),
            pltpu.SemaphoreType.DMA((4,)),
        ],
        compiler_params=PARAMS,
        cost_estimate=cost,
        name="early",
    )(me, *hbm)
    other = sent(apart, 1)
    early = [sent(pair, 2 * m) for pair, m in zip(pairs, early)]
    shapes = [blocks(1)] + [blocks(2)] * (across - 1)
    own, *joined = pl.pallas_call(
        functools.partial(rest_kernel, owners, capacity, echo_local),
        out_shape=shapes,
        in_specs=[SMEM] + [VMEM] * 5,
        out_specs=[VMEM] * len(shapes),
        scratch_shapes=scratch(across),
        compiler_params=PARAMS,
        cost_estimate=cost,
        name="rest",
    )(me, owner, slot, reduced, place, other)
    late = [sent(x, 2 * m) for x, m in zip(joined, late)]
    close = [sent(x, 2 * m) for x, m in zip(joined[len(late) :], close)]
    two = shares == 2
    flip = ((1 - mine) if two else jnp.zeros((), I32)).astype(I32).reshape(1)
    run = functools.partial(core_call, depth=depth, flip=flip, sampled=sampled, right=right)
    one, split, whole = ((0,), ()), ((0,), (1,)), ((0, 1), ())
    give, keep, *onward = run([own, other, *early], [one, one, *[split] * len(early)])
    onward = [sent(x, 1) for x in onward]
    total = run(close, [whole] * len(close), before=(give, keep))
    total = run(
        [*onward, *late[:-1]],
        [one] * len(onward) + [whole] * (len(late) - 1),
        before=total,
    )
    last = functools.partial(run, late[-1:], [whole])
    share = vox_local // shares
    if not two:
        both = jnp.concatenate(last(before=total), axis=1)
        both = both.reshape(FINE * rank, shares, FINE * rank // shares)
        both = lax.psum_scatter(both, "echo", scatter_dimension=1)
        both = both.reshape(FINE, rank, FINE // shares, rank).transpose(2, 0, 1, 3)
        return both.reshape(share, rank * rank).astype(BF16)
    (give,) = last(halves=(0,), before=total[:1], kinds=[BF16])
    got = lax.ppermute(give, "echo", [(0, 1), (1, 0)])
    (keep,) = last(halves=(1,), before=total[1:])
    return pl.pallas_call(
        functools.partial(finish_kernel, rank),
        out_shape=jax.ShapeDtypeStruct((share, rank * rank), BF16),
        in_specs=[VMEM, VMEM],
        out_specs=VMEM,
        scratch_shapes=[pltpu.VMEM((FINE * rank, LANES), F32)],
        compiler_params=PARAMS,
        name="finish",
    )(keep, got)


def solution(mesh):
    return jax.shard_map(
        on_device,
        mesh=mesh,
        in_specs=(
            P(("vox", "echo"), None),
            P(("vox", "echo"), None),
            P(("vox", "echo"), None),
            P("vox", "echo"),
            P(),
            P("echo", None),
        ),
        out_specs=P(("vox", "echo"), None),
        check_vma=False,
    )
```

```python
import functools

import jax
import jax.numpy as jnp
from jax import lax
from jax.experimental import pallas as pl
from jax.experimental.pallas import tpu as pltpu
from jax.sharding import PartitionSpec as P

LANES = 128
CHUNK = 512
STEP = 1024
FINE = 16
BF16 = jnp.bfloat16
F32 = jnp.float32
I32 = jnp.int32


def nt_dot(lhs, rhs):
    return lax.dot_general(
        lhs, rhs, (((1,), (1,)), ((), ())), preferred_element_type=F32
    )


def nn_dot(lhs, rhs):
    return lax.dot_general(
        lhs, rhs, (((1,), (0,)), ((), ())), preferred_element_type=F32
    )


def chip_masks(owners):
    chips = owners // 4
    far = range(chips, 2 * chips)
    return list(far[0::2]), list(far[1::2]), list(range(1, chips))


def place_rows(owners, me, owner_ref, place_ref):
    rows = owner_ref.shape[1]
    chunks = rows // CHUNK
    owner_range = lax.broadcasted_iota(I32, (owners, CHUNK), 0)
    hots = []
    for j in range(chunks):
        relative = owner_ref[:, j * CHUNK : (j + 1) * CHUNK] ^ me
        hots.append((owner_range == relative).astype(F32))
    hot = jnp.concatenate(hots, axis=0)
    before = lax.broadcasted_iota(I32, (CHUNK, CHUNK), 0) < lax.broadcasted_iota(
        I32, (CHUNK, CHUNK), 1
    )
    prefix = nn_dot(hot.astype(BF16), before.astype(F32).astype(BF16))
    carry = jnp.zeros((owners, 1), F32)
    for j in range(chunks):
        part = prefix[j * owners : (j + 1) * owners]
        place = jnp.sum((part + carry) * hots[j], axis=0, keepdims=True)
        place_ref[j] = place.astype(I32)
        carry = carry + jnp.sum(hots[j], axis=1, keepdims=True)


def put_rows(
    wanted, capacity, echo_local, me, reduced_ref, owner_ref, slot_ref, place_ref,
    slots, spread_ref, hot_ref, ids_ref,
):
    rank, rows = reduced_ref.shape
    count = len(slots)
    groups = capacity // LANES
    lane_range = lax.broadcasted_iota(I32, (LANES, STEP), 0).astype(F32).astype(BF16)
    group_range = lax.broadcasted_iota(I32, (8, STEP), 0)

    def level(row, height):
        return jnp.broadcast_to(row.astype(F32), (height, STEP)).astype(BF16)

    for j in range(rows // STEP):
        at = slice(j * STEP, (j + 1) * STEP)
        reduced = reduced_ref[:, at]
        relative = owner_ref[:, at] ^ me
        slot = slot_ref[:, at]
        place = jnp.concatenate(
            [place_ref[j * (STEP // CHUNK) + i] for i in range(STEP // CHUNK)], axis=1
        )
        group = place // LANES
        lane = level(place % LANES, LANES)
        lane_hot = jnp.where(lane_range == lane, BF16(1), BF16(0))
        group_b = level(group, LANES)
        for g in range(groups):
            hot_ref[g * LANES : (g + 1) * LANES, at] = jnp.where(
                group_b == BF16(g), lane_hot, BF16(0)
            )
        here = group_range == group
        voxel = jnp.where(here, (slot // echo_local).astype(F32), 0.0)
        echo = jnp.where(here, (slot % echo_local).astype(F32), 0.0)
        ids = jnp.concatenate([voxel, echo], axis=0).astype(BF16)
        owner_b = level(relative, rank)
        owner_c = level(relative, 16)
        for o in range(count):
            spread_ref[o * rank : (o + 1) * rank, at] = jnp.where(
                owner_b == BF16(wanted[o]), reduced, BF16(0)
            )
        spread_ids = jnp.concatenate(
            [
                jnp.where(owner_c == BF16(wanted[o]), ids, BF16(0))
                for o in range(count)
            ],
            axis=0,
        )
        part = nt_dot(spread_ids, lane_hot)
        ids_ref[...] = part if j == 0 else ids_ref[...] + part
    for o, (out_ref, base) in enumerate(slots):
        base += groups * rank
        out_ref[base : base + 16, :] = ids_ref[o * 16 : (o + 1) * 16, :].astype(BF16)
    wide = 2 * LANES
    for g in range(0, groups, 2):
        made = nt_dot(spread_ref[...], hot_ref[g * LANES : g * LANES + wide, :]).astype(BF16)
        for o, (out_ref, base) in enumerate(slots):
            for i in range(2):
                at = base + (g + i) * rank
                out_ref[at : at + rank, :] = made[
                    o * rank : (o + 1) * rank, i * LANES : (i + 1) * LANES
                ]


def early_kernel(
    owners, capacity, echo_local, me_ref, acquired_hbm, owner_hbm, slot_hbm, left_hbm,
    reduced_ref, place_ref, owner_ref, slot_ref, *refs,
):
    chips = owners // 4
    pairs, refs = refs[: chips // 2], refs[chips // 2 :]
    apart_ref, acquired_ref, left_ref, spread_ref, hot_ref, ids_ref, sems = refs
    depth = pairs[0].shape[0] // 2
    copies = [
        pltpu.make_async_copy(a, b, sems.at[i])
        for i, (a, b) in enumerate(
            [
                (owner_hbm, owner_ref),
                (slot_hbm, slot_ref),
                (acquired_hbm, acquired_ref),
                (left_hbm, left_ref),
            ]
        )
    ]
    for copy in copies:
        copy.start()
    copies[0].wait()
    me = me_ref[0]
    place_rows(owners, me, owner_ref, place_ref)
    for copy in copies[1:]:
        copy.wait()
    reduced_ref[...] = nt_dot(left_ref[...], acquired_ref[...]).astype(BF16)
    early, late, close = chip_masks(owners)
    wanted, slots = [], []
    for m, pair in zip(early, pairs):
        wanted += [2 * m, 2 * m + 1]
        slots += [(pair, 0), (pair, depth)]
    for i, m in enumerate([0, *late, *close]):
        wanted.append(2 * m + 1)
        slots.append((apart_ref, i * depth))
    put_rows(
        wanted, capacity, echo_local, me, reduced_ref, owner_ref, slot_ref, place_ref,
        slots, spread_ref, hot_ref, ids_ref,
    )


def rest_kernel(
    owners, capacity, echo_local, me_ref, owner_ref, slot_ref, reduced_ref, place_ref,
    other_ref, own_ref, *refs,
):
    _, late, close = chip_masks(owners)
    masks = [*late, *close]
    joined, scratch = refs[: len(masks)], refs[len(masks) :]
    depth = own_ref.shape[0]
    for i, ref in enumerate(joined):
        ref[depth:, :] = other_ref[(i + 1) * depth : (i + 2) * depth, :]
    put_rows(
        [0, *[2 * m for m in masks]], capacity, echo_local, me_ref[0],
        reduced_ref, owner_ref, slot_ref, place_ref,
        [(own_ref, 0), *[(ref, 0) for ref in joined]], *scratch,
    )


def core_kernel(
    plan, depth, halves, more, flip_ref, sampled_ref, right_ref, *refs
):
    arrays, refs = refs[: len(plan)], refs[len(plan) :]
    blocks = [(r, i * depth) for r, p in zip(arrays, plan) for i in p[0]]
    onward = [(r, i * depth) for r, p in zip(arrays, plan) for i in p[1]]
    before = refs[: len(halves)] if more else None
    refs = refs[len(halves) :] if more else refs
    outs, refs = refs[: len(halves)], refs[len(halves) :]
    if onward:
        for out_ref, (ref, base) in zip(refs, onward):
            out_ref[...] = ref[base : base + depth, :]
        refs = refs[len(onward) :]
    a_ref, b_ref = refs
    rank = right_ref.shape[0]
    groups = (depth - 16) // rank
    size = groups * LANES
    half = FINE // 2
    flip = flip_ref[0] * half
    echo_local = sampled_ref.shape[1]
    bits = sampled_ref[0:32, :]
    for b in range(1, sampled_ref.shape[0] // 32):
        bits = bits + (sampled_ref[b * 32 : (b + 1) * 32, :] << b)
    table = jnp.concatenate([right_ref[...], bits.astype(F32).astype(BF16)], axis=0)
    echo_range = lax.broadcasted_iota(I32, (echo_local, LANES), 0).astype(F32).astype(BF16)
    bit_range = lax.broadcasted_iota(I32, (32, LANES), 0)
    for s, (ref, base) in enumerate(blocks):
        ids = ref[base + groups * rank : base + depth, :].astype(F32)
        for g in range(groups):
            feature = ref[base + g * rank : base + (g + 1) * rank, :]
            voxel = ids[g : g + 1].astype(I32)
            echo = jnp.broadcast_to(ids[8 + g : 9 + g], (echo_local, LANES)).astype(BF16)
            echo_hot = jnp.where(echo == echo_range, BF16(1), BF16(0))
            found = nn_dot(table, echo_hot)
            word = jnp.sum(
                jnp.where(bit_range == voxel % 32, found[rank:], 0.0),
                axis=0, keepdims=True,
            ).astype(I32)
            mask = ((word >> (voxel // 32)) & 1).astype(F32)
            right = (found[:rank] * mask).astype(BF16)
            low = (voxel % FINE).astype(F32)
            high = ((voxel // FINE) ^ flip).astype(F32)
            low = jnp.broadcast_to(low, (rank, LANES)).astype(BF16)
            high = jnp.broadcast_to(high, (rank, LANES)).astype(BF16)
            at = slice(s * size + g * LANES, s * size + (g + 1) * LANES)
            for v in range(FINE):
                a_ref[v * rank : (v + 1) * rank, at] = jnp.where(
                    low == BF16(v), feature, BF16(0)
                )
            for h in halves:
                for v in range(half * h, half * (h + 1)):
                    w = v - half * halves[0]
                    b_ref[w * rank : (w + 1) * rank, at] = jnp.where(
                        high == BF16(v), right, BF16(0)
                    )
    for i in range(len(halves)):
        total = nt_dot(a_ref[...], b_ref[i * half * rank : (i + 1) * half * rank, :])
        if more:
            total = total + before[i][...]
        outs[i][...] = total.astype(outs[i].dtype)


def finish_kernel(rank, keep_ref, got_ref, out_ref, sum_ref):
    tiles = keep_ref.shape[1] // LANES
    per = LANES // rank
    block = lax.broadcasted_iota(I32, (FINE, LANES), 1) // rank
    for t in range(tiles):
        sum_ref[...] = (
            keep_ref[:, t * LANES : (t + 1) * LANES]
            + got_ref[:, t * LANES : (t + 1) * LANES].astype(F32)
        )
        for q in range(rank // per):
            rows = [
                sum_ref[pl.ds(q * per + i, FINE, stride=rank), :] for i in range(per)
            ]
            for k in range(per):
                made = None
                for i in range(per):
                    turn = (i - k) % per * rank
                    moved = pltpu.roll(rows[i], turn, 1) if turn else rows[i]
                    made = moved if made is None else jnp.where(block == i, moved, made)
                v = t * per + k
                out_ref[v * FINE : (v + 1) * FINE, q * LANES : (q + 1) * LANES] = (
                    made.astype(BF16)
                )


VMEM = pl.BlockSpec(memory_space=pltpu.VMEM)
SMEM = pl.BlockSpec(memory_space=pltpu.SMEM)
HBM = pl.BlockSpec(memory_space=pltpu.HBM)
PARAMS = pltpu.CompilerParams(vmem_limit_bytes=40 * 2**20)


def core_call(
    arrays, plan, depth, flip, sampled, right, halves=(0, 1), before=(), kinds=None
):
    rank = right.shape[0]
    groups = (depth - 16) // rank
    count = sum(len(p[0]) for p in plan)
    onward = sum(len(p[1]) for p in plan)
    rows = count * groups * LANES
    wide, narrow = FINE * rank, FINE * rank // 2
    first = 3 + len(arrays)
    kinds = kinds or [F32] * len(halves)
    shapes = [jax.ShapeDtypeStruct((wide, narrow), kind) for kind in kinds]
    shapes += [jax.ShapeDtypeStruct((depth, LANES), BF16)] * onward
    return pl.pallas_call(
        functools.partial(core_kernel, plan, depth, halves, bool(before)),
        out_shape=shapes,
        in_specs=[SMEM] + [VMEM] * (2 + len(arrays) + len(before)),
        out_specs=[VMEM] * len(shapes),
        scratch_shapes=[
            pltpu.VMEM((wide, rows), BF16),
            pltpu.VMEM((narrow * len(halves), rows), BF16),
        ],
        input_output_aliases={
            first + i: i for i in range(len(before)) if kinds[i] == F32
        },
        compiler_params=PARAMS,
        cost_estimate=pl.CostEstimate(flops=1, bytes_accessed=1, transcendentals=0),
        name="core",
    )(flip, sampled, right, *arrays, *before)


def on_device(acquired, owner, slot, sampled, left_panel, right_panel):
    owners = lax.axis_size("vox")
    shares = lax.axis_size("echo")
    rows = acquired.shape[0]
    capacity = 4 * rows // owners
    groups = capacity // LANES
    vox_local, echo_local = sampled.shape
    rank = left_panel.shape[1]
    depth = groups * rank + 16
    early, late, close = chip_masks(owners)
    me = lax.axis_index("vox").reshape(1)
    mine = lax.axis_index("echo")
    owner, slot = owner.reshape(1, rows), slot.reshape(1, rows)
    left, right = left_panel.T, right_panel.T

    def blocks(n):
        return jax.ShapeDtypeStruct((n * depth, LANES), BF16)

    def sent(array, mask):
        return lax.ppermute(array, "vox", [(i, i ^ mask) for i in range(owners)])

    def scratch(n):
        return [
            pltpu.VMEM((n * rank, rows), BF16),
            pltpu.VMEM((capacity, rows), BF16),
            pltpu.VMEM((n * 16, LANES), F32),
        ]

    cost = pl.CostEstimate(
        flops=rows * capacity * owners * rank,
        bytes_accessed=4 * rows * 128,
        transcendentals=0,
    )
    across = 1 + len(late) + len(close)
    shapes = [
        jax.ShapeDtypeStruct((rank, rows), BF16),
        jax.ShapeDtypeStruct((rows // CHUNK, 1, CHUNK), I32),
        jax.ShapeDtypeStruct(owner.shape, I32),
        jax.ShapeDtypeStruct(slot.shape, I32),
        *[blocks(2)] * len(early),
        blocks(across),
    ]
    hbm = [
        pltpu.with_memory_space_constraint(x, pltpu.HBM)
        for x in (acquired, owner, slot, left)
    ]
    reduced, place, owner, slot, *pairs, apart = pl.pallas_call(
        functools.partial(early_kernel, owners, capacity, echo_local),
        out_shape=shapes,
        in_specs=[SMEM, HBM, HBM, HBM, HBM],
        out_specs=[VMEM] * len(shapes),
        scratch_shapes=[
            pltpu.VMEM(acquired.shape, BF16),
            pltpu.VMEM(left.shape, BF16),
            *scratch(2 * len(early) + across),
            pltpu.SemaphoreType.DMA((4,)),
        ],
        compiler_params=PARAMS,
        cost_estimate=cost,
        name="early",
    )(me, *hbm)
    other = sent(apart, 1)
    early = [sent(pair, 2 * m) for pair, m in zip(pairs, early)]
    shapes = [blocks(1)] + [blocks(2)] * (across - 1)
    own, *joined = pl.pallas_call(
        functools.partial(rest_kernel, owners, capacity, echo_local),
        out_shape=shapes,
        in_specs=[SMEM] + [VMEM] * 5,
        out_specs=[VMEM] * len(shapes),
        scratch_shapes=scratch(across),
        compiler_params=PARAMS,
        cost_estimate=cost,
        name="rest",
    )(me, owner, slot, reduced, place, other)
    late = [sent(x, 2 * m) for x, m in zip(joined, late)]
    close = [sent(x, 2 * m) for x, m in zip(joined[len(late) :], close)]
    two = shares == 2
    flip = ((1 - mine) if two else jnp.zeros((), I32)).astype(I32).reshape(1)
    run = functools.partial(core_call, depth=depth, flip=flip, sampled=sampled, right=right)
    one, split, whole = ((0,), ()), ((0,), (1,)), ((0, 1), ())
    give, keep, *onward = run([own, other, *early], [one, one, *[split] * len(early)])
    onward = [sent(x, 1) for x in onward]
    total = run(close, [whole] * len(close), before=(give, keep))
    total = run(onward, [one] * len(onward), before=total)
    last = functools.partial(run, late, [whole] * len(late))
    share = vox_local // shares
    if not two:
        both = jnp.concatenate(last(before=total), axis=1)
        both = both.reshape(FINE * rank, shares, FINE * rank // shares)
        both = lax.psum_scatter(both, "echo", scatter_dimension=1)
        both = both.reshape(FINE, rank, FINE // shares, rank).transpose(2, 0, 1, 3)
        return both.reshape(share, rank * rank).astype(BF16)
    (give,) = last(halves=(0,), before=total[:1], kinds=[BF16])
    got = lax.ppermute(give, "echo", [(0, 1), (1, 0)])
    (keep,) = last(halves=(1,), before=total[1:])
    return pl.pallas_call(
        functools.partial(finish_kernel, rank),
        out_shape=jax.ShapeDtypeStruct((share, rank * rank), BF16),
        in_specs=[VMEM, VMEM],
        out_specs=VMEM,
        scratch_shapes=[pltpu.VMEM((FINE * rank, LANES), F32)],
        compiler_params=PARAMS,
        name="finish",
    )(keep, got)


def solution(mesh):
    return jax.shard_map(
        on_device,
        mesh=mesh,
        in_specs=(
            P(("vox", "echo"), None),
            P(("vox", "echo"), None),
            P(("vox", "echo"), None),
            P("vox", "echo"),
            P(),
            P("echo", None),
        ),
        out_specs=P(("vox", "echo"), None),
        check_vma=False,
    )
```
